512 devices in a mesh: gx: 16 (over z, core), gy: 8 (over y), gz: 4 (over x).
Axes of the slice: x: 4, y: 8, z: 8, core: 2. Of those that a mesh axis runs over, the one named last changes fastest.
Arguments:
- start: float32 [4, 80, 256, 512], P(None, 'gx', 'gy', 'gz'), may hold values from -6 to 6
- rhs_block: float32 [4, 80, 256, 512], P(None, 'gx', 'gy', 'gz'), may hold values from -6 to 6
- coefficients: float32 [4, 80, 256, 512], P(None, 'gx', 'gy', 'gz'), may hold values from 0.5 to 2
Outputs:
- solution: float32 [4, 80, 256, 512], P(None, 'gx', 'gy', 'gz')
The draws below stay inside these ranges and needn't reach their ends.
All inputs are finite; a program needn't handle non-finite values.
Results may differ from the reference program's by a relative error of at most 0.0003.
Values sent between devices are 32-bit elements; how exact they have to be, the bound alone decides.
A program may use at most 192 MiB of HBM per device.

```python
import jax
import jax.numpy as jnp
from jax import lax

NRHS = 4
S = 4
NX = 80
NY = 256
NZ = 512


def levels(stream_key, dims, shards, least, top_value):
    factor_of = 1.0
    for dim, shards_of in shards:
        heights = jax.random.uniform(jax.random.fold_in(jax.random.fold_in(stream_key, 6), dim), (shards_of,), jnp.float32, least / len(shards), top_value / len(shards))
        factor_of = factor_of * jnp.repeat(jnp.exp(heights), dims[dim] // shards_of).reshape((-1,) + (1,) * (len(dims) - 1 - dim))
    return factor_of


def normal_values(rng, shape, deviation, bound, shards=(), kind=jnp.bfloat16):
    array = deviation * jax.random.normal(rng, shape, jnp.float32)
    if shards:
        array = array * levels(rng, shape, shards, -0.22, 0.18)
    return jnp.clip(array, -bound, bound).astype(kind)


def setup_inputs(seed: int = 0) -> dict:
    arg_keys = jax.random.split(jax.random.key(seed), 4)
    return {
        "start": normal_values(arg_keys[0], (NRHS, NX, NY, NZ), 1.0, 6.0, ((1, 16), (2, 8), (3, 4)), jnp.float32),
        "rhs_block": normal_values(arg_keys[1], (NRHS, NX, NY, NZ), 1.0, 6.0, ((1, 16), (2, 8), (3, 4)), jnp.float32),
        "coefficients": jnp.clip(0.5 + 1.5 * jax.random.uniform(arg_keys[2], (4, NX, NY, NZ), jnp.float32) ** levels(arg_keys[2], (4, NX, NY, NZ), ((1, 16), (2, 8), (3, 4)), -0.2, 0.2), 0.5, 2.0),
    }


basis_shift = 8.75
basis_scale = 4.0

def stencil(field, coefs):
    center = field[:, 1:-1, 1:-1, 1:-1]
    result = coefs[0, 1:-1, 1:-1, 1:-1] * center
    result = result + coefs[1, 1:-1, 1:-1, 1:-1] * (center - field[:, 2:, 1:-1, 1:-1])
    result = result + coefs[1, :-2, 1:-1, 1:-1] * (center - field[:, :-2, 1:-1, 1:-1])
    result = result + coefs[2, 1:-1, 1:-1, 1:-1] * (center - field[:, 1:-1, 2:, 1:-1])
    result = result + coefs[2, 1:-1, :-2, 1:-1] * (center - field[:, 1:-1, :-2, 1:-1])
    result = result + coefs[3, 1:-1, 1:-1, 1:-1] * (center - field[:, 1:-1, 1:-1, 2:])
    result = result + coefs[3, 1:-1, 1:-1, :-2] * (center - field[:, 1:-1, 1:-1, :-2])
    return result

def operate(field, coefs):
    widths = ((0, 0), (1, 1), (1, 1), (1, 1))
    return stencil(jnp.pad(field, widths), jnp.pad(coefs, widths))

def reflect_rows(tall):
    count = tall.shape[0]
    entries = tall.shape[1]
    position = jnp.arange(entries)
    for j in range(count):
        column = jnp.where(position >= j, tall[j], 0.0)
        length = jnp.sqrt(jnp.sum(column * column))
        leading = tall[j, j]
        mirror = -jnp.where(leading >= 0, 1.0, -1.0) * length
        vector = column - mirror * (position == j).astype(jnp.float32)
        weight = jnp.sum(vector * vector)
        project = jnp.dot(tall, vector, precision=lax.Precision.HIGHEST) / weight
        tall = tall - 2.0 * project[:, None] * vector[None, :]
    factor = tall[:, :count].T
    flip_sign = jnp.where(jnp.diagonal(factor) >= 0, 1.0, -1.0)
    return jnp.triu(factor * flip_sign[:, None])

def back_solve(triangle, values):
    count = triangle.shape[0]
    answer = [None] * count
    for i in reversed(range(count)):
        partial_sum = values[i]
        for j in range(i + 1, count):
            partial_sum = partial_sum - triangle[i, j] * answer[j]
        answer[i] = partial_sum / triangle[i, i]
    return jnp.stack(answer)

def least_squares(upper, nrhs):
    total = upper.shape[0]
    kept = total - nrhs
    rows = jnp.arange(total)[:, None]
    cols = jnp.arange(kept)[None, :]
    shifts = basis_shift * (rows == cols).astype(jnp.float32) + basis_scale * (rows == cols + nrhs).astype(jnp.float32)
    mixed = jnp.dot(upper, shifts, precision=lax.Precision.HIGHEST)
    joined = jnp.concatenate([mixed, upper[:, :nrhs]], axis=1)
    reduced = reflect_rows(joined.T)
    return back_solve(reduced[:kept, :kept], reduced[:kept, kept:])

def reference(start, rhs_block, coefficients):
    nrhs = start.shape[0]
    blocks = [rhs_block - operate(start, coefficients)]
    for step in range(S):
        before = blocks[-1]
        blocks.append((operate(before, coefficients) - basis_shift * before) / basis_scale)
    tall = jnp.stack(blocks).reshape(len(blocks) * nrhs, -1)
    gram = jnp.dot(tall, tall.T, precision=lax.Precision.HIGHEST)
    upper = jnp.linalg.cholesky(gram).T
    weights = least_squares(upper, nrhs)
    kept = tall.shape[0] - nrhs
    update = jnp.dot(weights.T, tall[:kept], precision=lax.Precision.HIGHEST)
    return start + update.reshape(start.shape)
```

```python
import itertools

import jax
import jax.numpy as jnp
from jax import lax
from jax.experimental import pallas as pl
from jax.experimental.pallas import tpu as pltpu
from jax.sharding import PartitionSpec as P

MESH = pl.DeviceIdType.MESH
F32 = jnp.float32
HIGH = lax.Precision.HIGHEST
AXES = ("gx", "gy", "gz")
SHIFT, SCALE = 8.75, 4.0
PAIRS = [(i, j) for i in range(4) for j in range(i, 4)]
PLACE = {(i, j): PAIRS.index((min(i, j), max(i, j))) for i in range(4) for j in range(4)}
TOP = 8
XLO, XHI, YLO, YHI, ZLO, ZHI, CX = range(7)


def rolled(tile, shift):
    return pltpu.roll(tile, shift % 128, 1)


def kernel(
    sizes, start, rhs, coef, out,
    V, rhs_v, coef_v, bd, bc1, bc2, bc3p, bc3m, e3, e1, e2,
    xh, c1h, ys, yr, zs, zr, G, row_a, row_b, msg, rep, W,
    lsem, ssem, rsem, asem,
):
    nx, ny, nz = sizes
    me = [lax.axis_index(axis) for axis in AXES]

    def shifted(offset):
        return tuple(lax.rem(m + (d + s), s) for m, d, s in zip(me, offset, sizes))

    neighbours = [shifted(o) for o in ((1, 0, 0), (-1, 0, 0), (0, 1, 0), (0, -1, 0), (0, 0, 1), (0, 0, -1))]

    def far(o):
        return -sum(min(d, s - d) for d, s in zip(o, sizes))

    plane = sorted([(0, b, c) for b, c in itertools.product(range(ny), range(nz)) if b or c], key=far)
    line = sorted([(a, 0, 0) for a in range(1, nx)], key=far)

    loads = [
        pltpu.make_async_copy(start.at[f], V.at[0, :, f, pl.ds(TOP, 32), :], lsem.at[f]) for f in range(4)
    ] + [pltpu.make_async_copy(coef, coef_v, lsem.at[4]), pltpu.make_async_copy(rhs, rhs_v, lsem.at[5])]
    for copy in loads:
        copy.start()

    barrier = pltpu.get_barrier_semaphore()
    partners = [shifted(o) for o in plane + line]
    for partner in partners:
        pl.semaphore_signal(barrier, inc=1, device_id=partner, device_id_type=MESH)

    lane = lax.broadcasted_iota(jnp.int32, (8, 128), 1)
    sub = lax.broadcasted_iota(jnp.int32, (8, 128), 0)
    pair_lane = lax.shift_right_logical(lane, 1)
    even_lane = lax.rem(lane, 2) == 0
    zero = jnp.zeros((8, 128), F32)

    def inside(axis, edge):
        return jnp.where(me[axis] == edge, 0.0, 1.0).astype(F32)

    low = [inside(0, 0), inside(1, 0), inside(2, 0)]
    high = [inside(0, nx - 1), inside(1, ny - 1), inside(2, nz - 1)]

    def clear(i, carry):
        for f in range(4):
            for x in range(5):
                V[i, x, f, pl.ds(0, 8), :] = zero
                V[i, x, f, pl.ds(TOP + 32, 8), :] = zero
        return carry

    lax.fori_loop(0, 5, clear, 0)
    for x in range(5):
        bc2[x, pl.ds(0, 8), :] = zero
    G[pl.ds(96, 32), :] = jnp.zeros((32, 128), F32)

    loads[4].wait()

    for x in range(5):
        for t in range(4):
            rows = pl.ds(8 * t, 8)
            bc2[x, pl.ds(TOP + 8 * t, 8), :] = -0.25 * coef_v[2, x, rows, :]
        for t in range(4):
            rows = pl.ds(8 * t, 8)
            n1 = -0.25 * coef_v[1, x, rows, :]
            n3 = -0.25 * coef_v[3, x, rows, :]
            bc1[x, rows, :] = n1
            bc3p[x, rows, :] = jnp.where(lane == 127, 0.0, n3)
            back = jnp.where(lane == 0, 0.0, rolled(n3, 1))
            bc3m[x, rows, :] = back
            e3[x, rows, :] = jnp.where(lane == 127, n3 * high[2], 0.0)
            total = n1 + n3 + back + bc2[x, pl.ds(TOP + 8 * t, 8), :] + bc2[x, pl.ds(TOP - 1 + 8 * t, 8), :]
            if x > 0:
                total = total + bc1[x - 1, rows, :]
            bd[x, rows, :] = 0.25 * (coef_v[0, x, rows, :] - SHIFT) - total
            if x == 4:
                e1[1, rows, :] = n1 * high[0]
        e2[1, x, :, :] = jnp.where(sub == 7, bc2[x, pl.ds(TOP + 24, 8), :] * high[1], 0.0)

    def x_copies(p):
        return [
            pltpu.make_async_remote_copy(
                V.at[p, 4, :, pl.ds(TOP, 32), :], xh.at[p, 0], ssem.at[p, XLO], rsem.at[p, XLO],
                device_id=neighbours[0], device_id_type=MESH),
            pltpu.make_async_remote_copy(
                V.at[p, 0, :, pl.ds(TOP, 32), :], xh.at[p, 1], ssem.at[p, XHI], rsem.at[p, XHI],
                device_id=neighbours[1], device_id_type=MESH),
        ]

    def yz_copies(p):
        return [
            pltpu.make_async_remote_copy(
                ys.at[p, d], yr.at[p, d], ssem.at[p, YLO + d], rsem.at[p, YLO + d],
                device_id=neighbours[2 + d], device_id_type=MESH) for d in range(2)
        ] + [
            pltpu.make_async_remote_copy(
                zs.at[p], zr.at[p, d], ssem.at[p, ZLO + d], rsem.at[p, ZLO + d],
                device_id=neighbours[4 + d], device_id_type=MESH) for d in range(2)
        ]

    c_copy = pltpu.make_async_remote_copy(
        coef_v.at[1, 4], c1h, ssem.at[0, CX], rsem.at[0, CX], device_id=neighbours[0], device_id_type=MESH
    )

    def begin(copies):
        for copy in copies:
            copy.start()

    def pack(tile, spot, t, held):
        k = 2 * spot + t % 2
        held[t // 2] = jnp.where(pair_lane == k, rolled(tile, 2 * k + 1), held[t // 2])

    for copy in loads[:4]:
        copy.wait()
    held = [zero, zero]
    for x in range(5):
        for f in range(4):
            j = 4 * x + f
            ys[0, 0, pl.ds(j, 1), :] = V[0, x, f, pl.ds(TOP + 31, 1), :]
            ys[0, 1, pl.ds(j, 1), :] = V[0, x, f, pl.ds(TOP, 1), :]
            for t in range(4):
                pack(V[0, x, f, pl.ds(TOP + 8 * t, 8), :], j, t, held)
        ys[0, 0, pl.ds(20 + x, 1), :] = coef_v[2, x, pl.ds(31, 1), :]
        ys[0, 1, pl.ds(20 + x, 1), :] = coef_v[2, x, pl.ds(31, 1), :]
        for t in range(4):
            pack(coef_v[3, x, pl.ds(8 * t, 8), :], 20 + x, t, held)
    for h in range(2):
        zs[0, pl.ds(8 * h, 8), :] = held[h]

    pl.semaphore_wait(barrier, len(partners))
    begin(x_copies(0) + [c_copy] + yz_copies(0))

    def interior(p):
        def layer(x, below, above):
            for t in range(4):
                rows = pl.ds(8 * t, 8)
                c_d, c_xp = bd[x, rows, :], bc1[x, rows, :]
                c_yp, c_ym = bc2[x, pl.ds(TOP + 8 * t, 8), :], bc2[x, pl.ds(TOP - 1 + 8 * t, 8), :]
                c_zp, c_zm = bc3p[x, rows, :], bc3m[x, rows, :]
                for f in range(4):
                    v = V[p, x, f, pl.ds(TOP + 8 * t, 8), :]
                    total = c_d * v
                    total = total + c_yp * V[p, x, f, pl.ds(TOP + 1 + 8 * t, 8), :]
                    total = total + c_ym * V[p, x, f, pl.ds(TOP - 1 + 8 * t, 8), :]
                    if above:
                        total = total + c_xp * V[p, x + 1, f, pl.ds(TOP + 8 * t, 8), :]
                    if below:
                        total = total + bc1[x - 1, rows, :] * V[p, x - 1, f, pl.ds(TOP + 8 * t, 8), :]
                    total = total + c_zp * rolled(v, -1)
                    total = total + c_zm * rolled(v, 1)
                    V[p + 1, x, f, pl.ds(TOP + 8 * t, 8), :] = total

        layer(0, False, True)

        def middle(x, carry):
            layer(x, True, True)
            return carry

        lax.fori_loop(1, 4, middle, 0)
        layer(4, True, False)

    def products(p):
        def layer(x, sums):
            sums = list(sums)
            for t in range(4):
                new = [V[p, x, f, pl.ds(TOP + 8 * t, 8), :] for f in range(4)]
                old = [V[p - 1, x, f, pl.ds(TOP + 8 * t, 8), :] for f in range(4)]
                for q, (i, j) in enumerate(PAIRS):
                    sums[q] = sums[q] + old[i] * new[j]
                    sums[10 + q] = sums[10 + q] + new[i] * new[j]
            return tuple(sums)

        sums = lax.fori_loop(0, 5, layer, (zero,) * 20)
        for q in range(20):
            G[pl.ds(20 * p - 20 + q, 1), :] = jnp.sum(sums[q], axis=0, keepdims=True)

    def finish(p, first=False, last=False):
        for copy in x_copies(p) + yz_copies(p) + ([c_copy] if first else []):
            copy.wait_recv()
        both = [
            jnp.where(even_lane, zr[p, 0, pl.ds(8 * h, 8), :], rolled(zr[p, 1, pl.ds(8 * h, 8), :], -2))
            for h in range(2)
        ]
        held = [zero, zero]
        for x in (0, 4, 1, 2, 3):
            for t in range(4):
                rows = pl.ds(8 * t, 8)
                edge = e3[x, rows, :]
                if first:
                    k = 2 * (20 + x) + t % 2
                    more = jnp.where(lane == 0, (-0.25 * low[2]) * rolled(both[t // 2], -2 * k), 0.0)
                    edge = edge + more
                    e3[x, rows, :] = edge
                    if x == 0:
                        face = (-0.25 * low[0]) * c1h[rows, :]
                        e1[0, rows, :] = face
                        more = more + face
                    if t == 0:
                        row = jnp.broadcast_to(yr[p, 0, pl.ds(20 + x, 1), :], (8, 128))
                        face = jnp.where(sub == 0, (-0.25 * low[1]) * row, 0.0)
                        e2[0, x, :, :] = face
                        more = more + face
                    bd[x, rows, :] = bd[x, rows, :] - more
                for f in range(4):
                    j = 4 * x + f
                    k = 2 * j + t % 2
                    cells = pl.ds(TOP + 8 * t, 8)
                    total = V[p + 1, x, f, cells, :]
                    if x == 0:
                        total = total + e1[0, rows, :] * xh[p, 0, f, rows, :]
                    if x == 4:
                        total = total + e1[1, rows, :] * xh[p, 1, f, rows, :]
                    if t == 0:
                        total = total + e2[0, x, :, :] * jnp.broadcast_to(yr[p, 0, pl.ds(j, 1), :], (8, 128))
                    if t == 3:
                        total = total + e2[1, x, :, :] * jnp.broadcast_to(yr[p, 1, pl.ds(j, 1), :], (8, 128))
                    total = total + edge * rolled(both[t // 2], -2 * k)
                    if first:
                        v = V[p, x, f, cells, :]
                        total = total - more * v
                        total = rhs_v[f, x, rows, :] - SHIFT * v - SCALE * total
                    V[p + 1, x, f, cells, :] = total
                    if not last:
                        if t == 3:
                            ys[p + 1, 0, pl.ds(j, 1), :] = total[7:8, :]
                        if t == 0:
                            ys[p + 1, 1, pl.ds(j, 1), :] = total[0:1, :]
                        pack(total, j, t, held)
            if x == 4 and not last:
                begin(x_copies(p + 1))
        if not last:
            for h in range(2):
                zs[p + 1, pl.ds(8 * h, 8), :] = held[h]
            begin(yz_copies(p + 1))

    interior(0)
    loads[5].wait()
    finish(0, first=True)

    def power(p, carry):
        interior(p)
        products(p)
        finish(p)
        return carry

    lax.fori_loop(1, 4, power, 0)
    interior(4)
    products(4)
    finish(4, last=True)
    products(5)

    ones = jnp.ones((8, 128), F32)

    def everyone(row, offsets, rows_ref, mine, count, slot):
        msg[slot, :, :] = row
        copies = [
            pltpu.make_async_remote_copy(
                msg.at[slot, pl.ds(0, 1), :], rows_ref.at[pl.ds(mine, 1), :], asem.at[slot, 0], asem.at[slot, 1],
                device_id=shifted(o), device_id_type=MESH) for o in offsets
        ]
        begin(copies)
        others = rows_ref.at[pl.ds(0, count - 1), :]
        pltpu.make_async_copy(others, others, asem.at[slot, 1]).wait()
        total = None
        for r in range(count // 8):
            part = jnp.where(sub + 8 * r == mine, row, rows_ref[pl.ds(8 * r, 8), :])
            total = part if total is None else total + part
        return jnp.broadcast_to(jnp.sum(total, axis=0, keepdims=True), (8, 128))

    def sent(rows_ref, count, slot):
        others = rows_ref.at[pl.ds(0, count - 1), :]
        pltpu.make_async_copy(others, others, asem.at[slot, 0]).wait()

    g = lax.dot_general(ones, G[...], (((1,), (1,)), ((), ())), precision=HIGH, preferred_element_type=F32)
    g = everyone(g, plane, row_a, me[1] * nz + me[2], ny * nz, 0)
    g = everyone(g, line, row_b, me[0], nx, 1)

    ahead, after = rolled(g, -10), rolled(g, -20)
    normal = (SHIFT * SHIFT) * g + (2 * SHIFT * SCALE) * ahead + (SCALE * SCALE) * after
    right = SHIFT * g + SCALE * ahead
    entries = jnp.where(lane < 80, normal, rolled(right, 70))
    spread = jnp.concatenate([jnp.where(sub + 8 * r == lane, entries, 0.0) for r in range(16)], axis=0)
    rep[...] = lax.dot_general(
        spread, jnp.ones((128, 128), F32), (((1,), (0,)), ((), ())), precision=HIGH, preferred_element_type=F32
    )

    def entry(r):
        return jnp.broadcast_to(rep[pl.ds(r, 1), :], (8, 128))

    n = 16
    a = {}
    for i in range(n):
        for j in range(i + 1):
            a[i, j] = entry(10 * (i // 4 + j // 4 + 1) + PLACE[i % 4, j % 4])
    b = []
    for i in range(n):
        value = entry(80 + 10 * (i // 4) + PLACE[i % 4, 3])
        for j in range(3):
            value = jnp.where(sub == j, entry(80 + 10 * (i // 4) + PLACE[i % 4, j]), value)
        b.append(value)
    inverse = []
    for k in range(n):
        inverse.append(1.0 / a[k, k])
        for i in range(k + 1, n):
            factor = a[i, k] * inverse[k]
            for j in range(k + 1, i + 1):
                a[i, j] = a[i, j] - factor * a[j, k]
            b[i] = b[i] - factor * b[k]
    for i in reversed(range(n)):
        b[i] = b[i] * inverse[i]
        W[i, :, :] = b[i]
        for j in range(i):
            b[j] = b[j] - a[i, j] * b[i]

    def update(x, carry):
        total = [[V[0, x, f, pl.ds(TOP + 8 * t, 8), :] for t in range(4)] for f in range(4)]
        for c in range(16):
            v = [V[1 + c // 4, x, c % 4, pl.ds(TOP + 8 * t, 8), :] for t in range(4)]
            for f in range(4):
                w = jnp.broadcast_to(W[c, pl.ds(f, 1), :], (8, 128))
                for t in range(4):
                    total[f][t] = total[f][t] + w * v[t]
        for f in range(4):
            for t in range(4):
                out[f, x, pl.ds(8 * t, 8), :] = total[f][t]
        return carry

    lax.fori_loop(0, 5, update, 0)

    for p in range(5):
        for copy in x_copies(p) + yz_copies(p):
            copy.wait_send()
    c_copy.wait_send()
    sent(row_a, ny * nz, 0)
    sent(row_b, nx, 1)


def solution(mesh):
    sizes = tuple(mesh.shape[axis] for axis in AXES)
    spec = P(None, "gx", "gy", "gz")

    def local(start, rhs_block, coefficients):
        vmem = lambda *shape: pltpu.VMEM(shape, F32)
        return pl.pallas_call(
            lambda *refs: kernel(sizes, *refs),
            out_shape=jax.ShapeDtypeStruct(start.shape, F32),
            in_specs=[pl.BlockSpec(memory_space=pl.ANY)] * 3,
            out_specs=pl.BlockSpec(memory_space=pltpu.VMEM),
            scratch_shapes=[
                vmem(6, 5, 4, 48, 128), vmem(4, 5, 32, 128), vmem(4, 5, 32, 128),
                vmem(5, 32, 128), vmem(5, 32, 128), vmem(5, 48, 128),
                vmem(5, 32, 128), vmem(5, 32, 128), vmem(5, 32, 128),
                vmem(2, 32, 128), vmem(2, 5, 8, 128),
                vmem(5, 2, 4, 32, 128), vmem(32, 128),
                vmem(5, 2, 32, 128), vmem(5, 2, 32, 128), vmem(5, 16, 128), vmem(5, 2, 16, 128),
                vmem(128, 128), vmem(32, 128), vmem(16, 128), vmem(2, 8, 128), vmem(128, 128), vmem(16, 8, 128),
                pltpu.SemaphoreType.DMA((6,)), pltpu.SemaphoreType.DMA((5, 7)),
                pltpu.SemaphoreType.DMA((5, 7)), pltpu.SemaphoreType.DMA((2, 2)),
            ],
            compiler_params=pltpu.CompilerParams(
                collective_id=0, has_side_effects=True, vmem_limit_bytes=24 << 20
            ),
        )(start, rhs_block, coefficients)

    return jax.shard_map(local, mesh=mesh, in_specs=(spec,) * 3, out_specs=spec, check_vma=False)
```

```python
import itertools

import jax
import jax.numpy as jnp
from jax import lax
from jax.experimental import pallas as pl
from jax.experimental.pallas import tpu as pltpu
from jax.sharding import PartitionSpec as P

MESH = pl.DeviceIdType.MESH
F32 = jnp.float32
AXES = ("gx", "gy", "gz")
SHIFT, SCALE = 8.75, 4.0
PAIRS = [(i, j) for i in range(4) for j in range(i, 4)]
PLACE = {(i, j): PAIRS.index((min(i, j), max(i, j))) for i in range(4) for j in range(4)}
TOP = 8
XLO, XHI, YLO, YHI, ZLO, ZHI, CX = range(7)


def rolled(tile, shift):
    return pltpu.roll(tile, shift % 128, 1)


def lane_sums(x):
    high = x.astype(jnp.bfloat16)
    rest = x - high.astype(F32)
    middle = rest.astype(jnp.bfloat16)
    low = (rest - middle.astype(F32)).astype(jnp.bfloat16)
    terms = jnp.concatenate([low, middle, high], axis=1)
    return jnp.dot(terms, jnp.ones((384, 128), jnp.bfloat16), preferred_element_type=F32)


def kernel(
    sizes, start, rhs, coef, out,
    V, rhs_v, coef_v, bd, bc1, bc2, bc3p, bc3m, e3, e1, e2,
    xh, c1h, ys, yr, zs, zr, G, row_a, row_b, msg, rep, W,
    lsem, ssem, rsem, asem,
):
    nx, ny, nz = sizes
    me = [lax.axis_index(axis) for axis in AXES]

    def shifted(offset):
        return tuple(lax.rem(m + (d + s), s) for m, d, s in zip(me, offset, sizes))

    neighbours = [shifted(o) for o in ((1, 0, 0), (-1, 0, 0), (0, 1, 0), (0, -1, 0), (0, 0, 1), (0, 0, -1))]

    def far(o):
        return -sum(min(d, s - d) for d, s in zip(o, sizes))

    plane = sorted([(0, b, c) for b, c in itertools.product(range(ny), range(nz)) if b or c], key=far)
    line = sorted([(a, 0, 0) for a in range(1, nx)], key=far)

    loads = [
        pltpu.make_async_copy(start.at[f], V.at[0, :, f, pl.ds(TOP, 32), :], lsem.at[f]) for f in range(4)
    ] + [pltpu.make_async_copy(coef, coef_v, lsem.at[4]), pltpu.make_async_copy(rhs, rhs_v, lsem.at[5])]
    for copy in loads:
        copy.start()

    barrier = pltpu.get_barrier_semaphore()
    twin = me[0] + 1 - 2 * lax.rem(me[0], 2)
    near = [(twin, me[1], me[2])] + [
        (lax.rem(base + d, nx), me[1], me[2]) for base in (me[0], twin) for d in (2, nx - 2)
    ] + neighbours[2:]
    for partner in near:
        pl.semaphore_signal(barrier, inc=1, device_id=partner, device_id_type=MESH)

    lane = lax.broadcasted_iota(jnp.int32, (8, 128), 1)
    sub = lax.broadcasted_iota(jnp.int32, (8, 128), 0)
    pair_lane = lax.shift_right_logical(lane, 1)
    even_lane = lax.rem(lane, 2) == 0
    zero = jnp.zeros((8, 128), F32)

    def inside(axis, edge):
        return jnp.where(me[axis] == edge, 0.0, 1.0).astype(F32)

    low = [inside(0, 0), inside(1, 0), inside(2, 0)]
    high = [inside(0, nx - 1), inside(1, ny - 1), inside(2, nz - 1)]

    def x_copies(p):
        return [
            pltpu.make_async_remote_copy(
                V.at[p, 4, :, pl.ds(TOP, 32), :], xh.at[p, 0], ssem.at[p, XLO], rsem.at[p, XLO],
                device_id=neighbours[0], device_id_type=MESH),
            pltpu.make_async_remote_copy(
                V.at[p, 0, :, pl.ds(TOP, 32), :], xh.at[p, 1], ssem.at[p, XHI], rsem.at[p, XHI],
                device_id=neighbours[1], device_id_type=MESH),
        ]

    def yz_copies(p):
        return [
            pltpu.make_async_remote_copy(
                ys.at[p, d], yr.at[p, d], ssem.at[p, YLO + d], rsem.at[p, YLO + d],
                device_id=neighbours[2 + d], device_id_type=MESH) for d in range(2)
        ] + [
            pltpu.make_async_remote_copy(
                zs.at[p], zr.at[p, d], ssem.at[p, ZLO + d], rsem.at[p, ZLO + d],
                device_id=neighbours[4 + d], device_id_type=MESH) for d in range(2)
        ]

    c_copy = pltpu.make_async_remote_copy(
        coef_v.at[1, 4], c1h, ssem.at[0, CX], rsem.at[0, CX], device_id=neighbours[0], device_id_type=MESH
    )

    def begin(copies):
        for copy in copies:
            copy.start()

    def pack(tile, spot, t, held):
        k = 2 * spot + t % 2
        held[t // 2] = jnp.where(pair_lane == k, rolled(tile, 2 * k + 1), held[t // 2])

    for copy in loads[:5]:
        copy.wait()
    held = [zero, zero]
    for x in range(5):
        for f in range(4):
            j = 4 * x + f
            ys[0, 0, pl.ds(j, 1), :] = V[0, x, f, pl.ds(TOP + 31, 1), :]
            ys[0, 1, pl.ds(j, 1), :] = V[0, x, f, pl.ds(TOP, 1), :]
            for t in range(4):
                pack(V[0, x, f, pl.ds(TOP + 8 * t, 8), :], j, t, held)
        ys[0, 0, pl.ds(20 + x, 1), :] = coef_v[2, x, pl.ds(31, 1), :]
        ys[0, 1, pl.ds(20 + x, 1), :] = coef_v[2, x, pl.ds(31, 1), :]
        for t in range(4):
            pack(coef_v[3, x, pl.ds(8 * t, 8), :], 20 + x, t, held)
    for h in range(2):
        zs[0, pl.ds(8 * h, 8), :] = held[h]

    pl.semaphore_wait(barrier, len(near))
    begin(x_copies(0) + [c_copy] + yz_copies(0))

    def clear(i, carry):
        for f in range(4):
            for x in range(5):
                V[i, x, f, pl.ds(0, 8), :] = zero
                V[i, x, f, pl.ds(TOP + 32, 8), :] = zero
        return carry

    lax.fori_loop(0, 5, clear, 0)
    for x in range(5):
        bc2[x, pl.ds(0, 8), :] = zero
    G[...] = zero

    for x in range(5):
        for t in range(4):
            rows = pl.ds(8 * t, 8)
            bc2[x, pl.ds(TOP + 8 * t, 8), :] = -0.25 * coef_v[2, x, rows, :]
        for t in range(4):
            rows = pl.ds(8 * t, 8)
            n1 = -0.25 * coef_v[1, x, rows, :]
            n3 = -0.25 * coef_v[3, x, rows, :]
            bc1[x, rows, :] = n1
            bc3p[x, rows, :] = jnp.where(lane == 127, 0.0, n3)
            back = jnp.where(lane == 0, 0.0, rolled(n3, 1))
            bc3m[x, rows, :] = back
            e3[x, rows, :] = jnp.where(lane == 127, n3 * high[2], 0.0)
            total = n1 + n3 + back + bc2[x, pl.ds(TOP + 8 * t, 8), :] + bc2[x, pl.ds(TOP - 1 + 8 * t, 8), :]
            if x > 0:
                total = total + bc1[x - 1, rows, :]
            bd[x, rows, :] = 0.25 * (coef_v[0, x, rows, :] - SHIFT) - total
            if x == 4:
                e1[1, rows, :] = n1 * high[0]
        e2[1, x, :, :] = jnp.where(sub == 7, bc2[x, pl.ds(TOP + 24, 8), :] * high[1], 0.0)

    def interior(p):
        def layer(x, below, above):
            for t in range(4):
                rows = pl.ds(8 * t, 8)
                c_d, c_xp = bd[x, rows, :], bc1[x, rows, :]
                c_yp, c_ym = bc2[x, pl.ds(TOP + 8 * t, 8), :], bc2[x, pl.ds(TOP - 1 + 8 * t, 8), :]
                c_zp, c_zm = bc3p[x, rows, :], bc3m[x, rows, :]
                for f in range(4):
                    v = V[p, x, f, pl.ds(TOP + 8 * t, 8), :]
                    total = c_d * v
                    total = total + c_yp * V[p, x, f, pl.ds(TOP + 1 + 8 * t, 8), :]
                    total = total + c_ym * V[p, x, f, pl.ds(TOP - 1 + 8 * t, 8), :]
                    if above:
                        total = total + c_xp * V[p, x + 1, f, pl.ds(TOP + 8 * t, 8), :]
                    if below:
                        total = total + bc1[x - 1, rows, :] * V[p, x - 1, f, pl.ds(TOP + 8 * t, 8), :]
                    total = total + c_zp * rolled(v, -1)
                    total = total + c_zm * rolled(v, 1)
                    V[p + 1, x, f, pl.ds(TOP + 8 * t, 8), :] = total

        layer(0, False, True)

        def middle(x, carry):
            layer(x, True, True)
            return carry

        lax.fori_loop(1, 4, middle, 0)
        layer(4, True, False)

    def products(p):
        def layer(x, sums):
            sums = list(sums)
            for t in range(4):
                new = [V[p, x, f, pl.ds(TOP + 8 * t, 8), :] for f in range(4)]
                old = [V[p - 1, x, f, pl.ds(TOP + 8 * t, 8), :] for f in range(4)]
                for q, (i, j) in enumerate(PAIRS):
                    sums[q] = sums[q] + old[i] * new[j]
                    sums[10 + q] = sums[10 + q] + new[i] * new[j]
            return tuple(sums)

        sums = lax.fori_loop(0, 5, layer, (zero,) * 20)
        totals = lane_sums(jnp.concatenate(sums, axis=0))
        block = G[...]
        for q in range(20):
            block = jnp.where(lane == 20 * p - 20 + q, totals[8 * q : 8 * q + 8, :], block)
        G[...] = block

    def finish(p, first=False, last=False):
        for copy in x_copies(p) + yz_copies(p) + ([c_copy] if first else []):
            copy.wait_recv()
        both = [
            jnp.where(even_lane, zr[p, 0, pl.ds(8 * h, 8), :], rolled(zr[p, 1, pl.ds(8 * h, 8), :], -2))
            for h in range(2)
        ]
        held = [zero, zero]
        for x in (0, 4, 1, 2, 3):
            for t in range(4):
                rows = pl.ds(8 * t, 8)
                edge = e3[x, rows, :]
                if first:
                    k = 2 * (20 + x) + t % 2
                    more = jnp.where(lane == 0, (-0.25 * low[2]) * rolled(both[t // 2], -2 * k), 0.0)
                    edge = edge + more
                    e3[x, rows, :] = edge
                    if x == 0:
                        face = (-0.25 * low[0]) * c1h[rows, :]
                        e1[0, rows, :] = face
                        more = more + face
                    if t == 0:
                        row = jnp.broadcast_to(yr[p, 0, pl.ds(20 + x, 1), :], (8, 128))
                        face = jnp.where(sub == 0, (-0.25 * low[1]) * row, 0.0)
                        e2[0, x, :, :] = face
                        more = more + face
                    bd[x, rows, :] = bd[x, rows, :] - more
                for f in range(4):
                    j = 4 * x + f
                    k = 2 * j + t % 2
                    cells = pl.ds(TOP + 8 * t, 8)
                    total = V[p + 1, x, f, cells, :]
                    if x == 0:
                        total = total + e1[0, rows, :] * xh[p, 0, f, rows, :]
                    if x == 4:
                        total = total + e1[1, rows, :] * xh[p, 1, f, rows, :]
                    if t == 0:
                        total = total + e2[0, x, :, :] * jnp.broadcast_to(yr[p, 0, pl.ds(j, 1), :], (8, 128))
                    if t == 3:
                        total = total + e2[1, x, :, :] * jnp.broadcast_to(yr[p, 1, pl.ds(j, 1), :], (8, 128))
                    total = total + edge * rolled(both[t // 2], -2 * k)
                    if first:
                        v = V[p, x, f, cells, :]
                        total = total - more * v
                        total = rhs_v[f, x, rows, :] - SHIFT * v - SCALE * total
                    V[p + 1, x, f, cells, :] = total
                    if not last:
                        if t == 3:
                            ys[p + 1, 0, pl.ds(j, 1), :] = total[7:8, :]
                        if t == 0:
                            ys[p + 1, 1, pl.ds(j, 1), :] = total[0:1, :]
                        pack(total, j, t, held)
            if x == 4 and not last:
                begin(x_copies(p + 1))
        if not last:
            for h in range(2):
                zs[p + 1, pl.ds(8 * h, 8), :] = held[h]
            begin(yz_copies(p + 1))

    interior(0)
    loads[5].wait()
    finish(0, first=True)

    def power(p, carry):
        interior(p)
        products(p)
        finish(p)
        return carry

    lax.fori_loop(1, 4, power, 0)
    interior(4)
    products(4)
    finish(4, last=True)
    products(5)

    def everyone(row, offsets, rows_ref, mine, count, slot):
        msg[slot, :, :] = row
        copies = [
            pltpu.make_async_remote_copy(
                msg.at[slot, pl.ds(0, 1), :], rows_ref.at[pl.ds(mine, 1), :], asem.at[slot, 0], asem.at[slot, 1],
                device_id=shifted(o), device_id_type=MESH) for o in offsets
        ]
        begin(copies)
        others = rows_ref.at[pl.ds(0, count - 1), :]
        pltpu.make_async_copy(others, others, asem.at[slot, 1]).wait()
        total = None
        for r in range(count // 8):
            part = jnp.where(sub + 8 * r == mine, row, rows_ref[pl.ds(8 * r, 8), :])
            total = part if total is None else total + part
        return jnp.broadcast_to(jnp.sum(total, axis=0, keepdims=True), (8, 128))

    def sent(rows_ref, count, slot):
        others = rows_ref.at[pl.ds(0, count - 1), :]
        pltpu.make_async_copy(others, others, asem.at[slot, 0]).wait()

    g = jnp.broadcast_to(jnp.sum(G[...], axis=0, keepdims=True), (8, 128))
    g = everyone(g, plane, row_a, me[1] * nz + me[2], ny * nz, 0)
    g = everyone(g, line, row_b, me[0], nx, 1)

    ahead, after = rolled(g, -10), rolled(g, -20)
    normal = (SHIFT * SHIFT) * g + (2 * SHIFT * SCALE) * ahead + (SCALE * SCALE) * after
    right = SHIFT * g + SCALE * ahead
    entries = jnp.where(lane < 80, normal, rolled(right, 70))
    spread = jnp.concatenate([jnp.where(sub + 8 * r == lane, entries, 0.0) for r in range(16)], axis=0)
    rep[...] = lane_sums(spread)

    def entry(r):
        return jnp.broadcast_to(rep[pl.ds(r, 1), :], (8, 128))

    n = 16
    a = {}
    for i in range(n):
        for j in range(i + 1):
            a[i, j] = entry(10 * (i // 4 + j // 4 + 1) + PLACE[i % 4, j % 4])
    b = []
    for i in range(n):
        value = entry(80 + 10 * (i // 4) + PLACE[i % 4, 3])
        for j in range(3):
            value = jnp.where(sub == j, entry(80 + 10 * (i // 4) + PLACE[i % 4, j]), value)
        b.append(value)
    inverse = []
    for k in range(n):
        inverse.append(1.0 / a[k, k])
        for i in range(k + 1, n):
            factor = a[i, k] * inverse[k]
            for j in range(k + 1, i + 1):
                a[i, j] = a[i, j] - factor * a[j, k]
            b[i] = b[i] - factor * b[k]
    for i in reversed(range(n)):
        b[i] = b[i] * inverse[i]
        W[i, :, :] = b[i]
        for j in range(i):
            b[j] = b[j] - a[i, j] * b[i]

    def update(x, carry):
        total = [[V[0, x, f, pl.ds(TOP + 8 * t, 8), :] for t in range(4)] for f in range(4)]
        for c in range(16):
            v = [V[1 + c // 4, x, c % 4, pl.ds(TOP + 8 * t, 8), :] for t in range(4)]
            for f in range(4):
                w = jnp.broadcast_to(W[c, pl.ds(f, 1), :], (8, 128))
                for t in range(4):
                    total[f][t] = total[f][t] + w * v[t]
        for f in range(4):
            for t in range(4):
                out[f, x, pl.ds(8 * t, 8), :] = total[f][t]
        return carry

    lax.fori_loop(0, 5, update, 0)

    for p in range(5):
        for copy in x_copies(p) + yz_copies(p):
            copy.wait_send()
    c_copy.wait_send()
    sent(row_a, ny * nz, 0)
    sent(row_b, nx, 1)


def solution(mesh):
    sizes = tuple(mesh.shape[axis] for axis in AXES)
    spec = P(None, "gx", "gy", "gz")

    def local(start, rhs_block, coefficients):
        vmem = lambda *shape: pltpu.VMEM(shape, F32)
        return pl.pallas_call(
            lambda *refs: kernel(sizes, *refs),
            out_shape=jax.ShapeDtypeStruct(start.shape, F32),
            in_specs=[pl.BlockSpec(memory_space=pl.ANY)] * 3,
            out_specs=pl.BlockSpec(memory_space=pltpu.VMEM),
            scratch_shapes=[
                vmem(6, 5, 4, 48, 128), vmem(4, 5, 32, 128), vmem(4, 5, 32, 128),
                vmem(5, 32, 128), vmem(5, 32, 128), vmem(5, 48, 128),
                vmem(5, 32, 128), vmem(5, 32, 128), vmem(5, 32, 128),
                vmem(2, 32, 128), vmem(2, 5, 8, 128),
                vmem(5, 2, 4, 32, 128), vmem(32, 128),
                vmem(5, 2, 32, 128), vmem(5, 2, 32, 128), vmem(5, 16, 128), vmem(5, 2, 16, 128),
                vmem(8, 128), vmem(32, 128), vmem(16, 128), vmem(2, 8, 128), vmem(128, 128), vmem(16, 8, 128),
                pltpu.SemaphoreType.DMA((6,)), pltpu.SemaphoreType.DMA((5, 7)),
                pltpu.SemaphoreType.DMA((5, 7)), pltpu.SemaphoreType.DMA((2, 2)),
            ],
            compiler_params=pltpu.CompilerParams(
                collective_id=0, has_side_effects=True, vmem_limit_bytes=60 << 20
            ),
        )(start, rhs_block, coefficients)

    return jax.shard_map(local, mesh=mesh, in_specs=(spec,) * 3, out_specs=spec, check_vma=False)
```

```python
import itertools

import jax
import jax.numpy as jnp
from jax import lax
from jax.experimental import pallas as pl
from jax.experimental.pallas import tpu as pltpu
from jax.sharding import PartitionSpec as P

MESH = pl.DeviceIdType.MESH
F32 = jnp.float32
AXES = ("gx", "gy", "gz")
SHIFT, SCALE = 8.75, 4.0
PAIRS = [(i, j) for i in range(4) for j in range(i, 4)]
PLACE = {(i, j): PAIRS.index((min(i, j), max(i, j))) for i in range(4) for j in range(4)}
TOP = 8
XLO, XHI, YLO, YHI, ZLO, ZHI = range(6)
YF, ZF = 8, 10


def rolled(tile, shift):
    return pltpu.roll(tile, shift % 128, 1)


def lane_sums(x):
    high = x.astype(jnp.bfloat16)
    rest = x - high.astype(F32)
    middle = rest.astype(jnp.bfloat16)
    low = (rest - middle.astype(F32)).astype(jnp.bfloat16)
    terms = jnp.concatenate([low, middle, high], axis=1)
    return jnp.dot(terms, jnp.ones((384, 128), jnp.bfloat16), preferred_element_type=F32)


def kernel(
    sizes, start, rhs, coef, out,
    V, rhs_v, coef_v, bd, bc1, bc2, bc3p, bc3m, e3, e1, e2,
    faces, c1h, ys, zs, G, parts, row_a, row_b, msg, rep, W,
    lsem, ssem, rsem, asem,
):
    nx, ny, nz = sizes
    me = [lax.axis_index(axis) for axis in AXES]

    def ahead_by(axis, d):
        place = me[axis] + d
        return place if d == 0 else jnp.where(place >= sizes[axis], place - sizes[axis], place)

    places = [[ahead_by(axis, d) for d in range(sizes[axis])] for axis in range(3)]

    def shifted(offset):
        return tuple(places[axis][d % sizes[axis]] for axis, d in enumerate(offset))

    neighbours = [shifted(o) for o in ((1, 0, 0), (-1, 0, 0), (0, 1, 0), (0, -1, 0), (0, 0, 1), (0, 0, -1))]

    def far(o):
        return -sum(min(d, s - d) for d, s in zip(o, sizes))

    plane = sorted([(0, b, c) for b, c in itertools.product(range(ny), range(nz)) if b or c], key=far)
    line = sorted([(a, 0, 0) for a in range(1, nx)], key=far)

    barrier = pltpu.get_barrier_semaphore()
    twin = me[0] + 1 - 2 * lax.rem(me[0], 2)
    near = [(twin, me[1], me[2])] + [
        (jnp.where(base + d >= nx, base + d - nx, base + d), me[1], me[2]) for base in (me[0], twin) for d in (2, nx - 2)
    ] + neighbours[2:]
    for partner in near:
        pl.semaphore_signal(barrier, inc=1, device_id=partner, device_id_type=MESH)

    loads = [
        pltpu.make_async_copy(start.at[f], V.at[0, :, f, pl.ds(TOP, 32), :], lsem.at[f]) for f in range(4)
    ] + [pltpu.make_async_copy(coef, coef_v, lsem.at[4]), pltpu.make_async_copy(rhs, rhs_v, lsem.at[5])]
    for copy in loads:
        copy.start()

    lane = lax.broadcasted_iota(jnp.int32, (8, 128), 1)
    sub = lax.broadcasted_iota(jnp.int32, (8, 128), 0)
    pair_lane = lax.shift_right_logical(lane, 1)
    even_lane = lax.rem(lane, 2) == 0
    zero = jnp.zeros((8, 128), F32)

    def inside(axis, edge):
        return jnp.where(me[axis] == edge, 0.0, 1.0).astype(F32)

    low = [inside(0, 0), inside(1, 0), inside(2, 0)]
    high = [inside(0, nx - 1), inside(1, ny - 1), inside(2, nz - 1)]

    def send(source, target, p, way):
        return pltpu.make_async_remote_copy(
            source, target, ssem.at[p], rsem.at[p], device_id=neighbours[way], device_id_type=MESH
        )

    def x_copies(p):
        return [
            send(V.at[p, 4 - 4 * d, :, pl.ds(TOP, 32), :], faces.at[p, pl.ds(4 * d, 4)], p, XLO + d) for d in range(2)
        ]

    def yz_copies(p):
        return [send(ys.at[p, d], faces.at[p, YF + d], p, YLO + d) for d in range(2)] + [
            send(zs.at[p], faces.at[p, ZF, pl.ds(16 * d, 16), :], p, ZLO + d) for d in range(2)
        ]

    def all_six(p, sem):
        pltpu.make_async_copy(faces.at[p], faces.at[p], sem.at[p]).wait()

    c_copy = pltpu.make_async_remote_copy(
        coef_v.at[1, 4], c1h, ssem.at[5], rsem.at[5], device_id=neighbours[0], device_id_type=MESH
    )

    def begin(copies):
        for copy in copies:
            copy.start()

    def pack(tile, spot, t, held):
        k = 2 * spot + t % 2
        held[t // 2] = jnp.where(pair_lane == k, rolled(tile, 2 * k + 1), held[t // 2])

    for copy in loads[:5]:
        copy.wait()
    held = [zero, zero]
    for x in range(5):
        for f in range(4):
            j = 4 * x + f
            ys[0, 0, pl.ds(j, 1), :] = V[0, x, f, pl.ds(TOP + 31, 1), :]
            ys[0, 1, pl.ds(j, 1), :] = V[0, x, f, pl.ds(TOP, 1), :]
            for t in range(4):
                pack(V[0, x, f, pl.ds(TOP + 8 * t, 8), :], j, t, held)
        ys[0, 0, pl.ds(20 + x, 1), :] = coef_v[2, x, pl.ds(31, 1), :]
        ys[0, 1, pl.ds(20 + x, 1), :] = coef_v[2, x, pl.ds(31, 1), :]
        for t in range(4):
            pack(coef_v[3, x, pl.ds(8 * t, 8), :], 20 + x, t, held)
    for h in range(2):
        zs[0, pl.ds(8 * h, 8), :] = held[h]

    pl.semaphore_wait(barrier, len(near))
    begin(x_copies(0) + [c_copy] + yz_copies(0))

    def clear(i, carry):
        for f in range(4):
            for x in range(5):
                V[i, x, f, pl.ds(0, 8), :] = zero
                V[i, x, f, pl.ds(TOP + 32, 8), :] = zero
        return carry

    lax.fori_loop(0, 5, clear, 0)
    for x in range(5):
        bc2[x, pl.ds(0, 8), :] = zero
    G[...] = zero
    parts[pl.ds(160, 32), :] = jnp.zeros((32, 128), F32)

    for x in range(5):
        for t in range(4):
            rows = pl.ds(8 * t, 8)
            bc2[x, pl.ds(TOP + 8 * t, 8), :] = -0.25 * coef_v[2, x, rows, :]
        for t in range(4):
            rows = pl.ds(8 * t, 8)
            n1 = -0.25 * coef_v[1, x, rows, :]
            n3 = -0.25 * coef_v[3, x, rows, :]
            bc1[x, rows, :] = n1
            bc3p[x, rows, :] = jnp.where(lane == 127, 0.0, n3)
            back = jnp.where(lane == 0, 0.0, rolled(n3, 1))
            bc3m[x, rows, :] = back
            e3[x, rows, :] = jnp.where(lane == 127, n3 * high[2], 0.0)
            total = n1 + n3 + back + bc2[x, pl.ds(TOP + 8 * t, 8), :] + bc2[x, pl.ds(TOP - 1 + 8 * t, 8), :]
            if x > 0:
                total = total + bc1[x - 1, rows, :]
            bd[x, rows, :] = 0.25 * (coef_v[0, x, rows, :] - SHIFT) - total
            if x == 4:
                e1[1, rows, :] = n1 * high[0]
        e2[1, x, :, :] = jnp.where(sub == 7, bc2[x, pl.ds(TOP + 24, 8), :] * high[1], 0.0)

    def interior(p):
        def layer(x, below, above):
            for t in range(4):
                rows = pl.ds(8 * t, 8)
                c_d, c_xp = bd[x, rows, :], bc1[x, rows, :]
                c_yp, c_ym = bc2[x, pl.ds(TOP + 8 * t, 8), :], bc2[x, pl.ds(TOP - 1 + 8 * t, 8), :]
                c_zp, c_zm = bc3p[x, rows, :], bc3m[x, rows, :]
                for f in range(4):
                    v = V[p, x, f, pl.ds(TOP + 8 * t, 8), :]
                    total = c_d * v
                    total = total + c_yp * V[p, x, f, pl.ds(TOP + 1 + 8 * t, 8), :]
                    total = total + c_ym * V[p, x, f, pl.ds(TOP - 1 + 8 * t, 8), :]
                    if above:
                        total = total + c_xp * V[p, x + 1, f, pl.ds(TOP + 8 * t, 8), :]
                    if below:
                        total = total + bc1[x - 1, rows, :] * V[p, x - 1, f, pl.ds(TOP + 8 * t, 8), :]
                    total = total + c_zp * rolled(v, -1)
                    total = total + c_zm * rolled(v, 1)
                    V[p + 1, x, f, pl.ds(TOP + 8 * t, 8), :] = total

        layer(0, False, True)

        def middle(x, carry):
            layer(x, True, True)
            return carry

        lax.fori_loop(1, 4, middle, 0)
        layer(4, True, False)

    def products(p):
        def layer(x, sums):
            sums = list(sums)
            for t in range(4):
                new = [V[p, x, f, pl.ds(TOP + 8 * t, 8), :] for f in range(4)]
                old = [V[p - 1, x, f, pl.ds(TOP + 8 * t, 8), :] for f in range(4)]
                for q, (i, j) in enumerate(PAIRS):
                    sums[q] = sums[q] + old[i] * new[j]
                    sums[10 + q] = sums[10 + q] + new[i] * new[j]
            return tuple(sums)

        sums = lax.fori_loop(0, 5, layer, (zero,) * 20)
        for q in range(20):
            parts[pl.ds(8 * q, 8), :] = sums[q]
        rows = parts[pl.ds(0, 24, stride=8), :]
        for r in range(1, 8):
            rows = rows + parts[pl.ds(r, 24, stride=8), :]
        totals = lane_sums(rows)
        block = G[...]
        for h in range(3):
            mine = lane == sub + (20 * p - 20 + 8 * h)
            if h == 2:
                mine = mine & (sub < 4)
            block = block + jnp.where(mine, totals[8 * h : 8 * h + 8, :], 0.0)
        G[...] = block

    def finish(p, first=False, last=False):
        all_six(p, rsem)
        if first:
            c_copy.wait_recv()
        both = [
            jnp.where(even_lane, faces[p, ZF, pl.ds(8 * h, 8), :], rolled(faces[p, ZF, pl.ds(16 + 8 * h, 8), :], -2))
            for h in range(2)
        ]
        held = [zero, zero]
        for x in (0, 4, 1, 2, 3):
            for t in range(4):
                rows = pl.ds(8 * t, 8)
                edge = e3[x, rows, :]
                if first:
                    k = 2 * (20 + x) + t % 2
                    more = jnp.where(lane == 0, (-0.25 * low[2]) * rolled(both[t // 2], -2 * k), 0.0)
                    edge = edge + more
                    e3[x, rows, :] = edge
                    if x == 0:
                        face = (-0.25 * low[0]) * c1h[rows, :]
                        e1[0, rows, :] = face
                        more = more + face
                    if t == 0:
                        row = jnp.broadcast_to(faces[p, YF, pl.ds(20 + x, 1), :], (8, 128))
                        face = jnp.where(sub == 0, (-0.25 * low[1]) * row, 0.0)
                        e2[0, x, :, :] = face
                        more = more + face
                    bd[x, rows, :] = bd[x, rows, :] - more
                for f in range(4):
                    j = 4 * x + f
                    k = 2 * j + t % 2
                    cells = pl.ds(TOP + 8 * t, 8)
                    total = V[p + 1, x, f, cells, :]
                    if x == 0:
                        total = total + e1[0, rows, :] * faces[p, f, rows, :]
                    if x == 4:
                        total = total + e1[1, rows, :] * faces[p, 4 + f, rows, :]
                    if t == 0:
                        total = total + e2[0, x, :, :] * jnp.broadcast_to(faces[p, YF, pl.ds(j, 1), :], (8, 128))
                    if t == 3:
                        total = total + e2[1, x, :, :] * jnp.broadcast_to(faces[p, YF + 1, pl.ds(j, 1), :], (8, 128))
                    total = total + edge * rolled(both[t // 2], -2 * k)
                    if first:
                        v = V[p, x, f, cells, :]
                        total = total - more * v
                        total = rhs_v[f, x, rows, :] - SHIFT * v - SCALE * total
                    V[p + 1, x, f, cells, :] = total
                    if not last:
                        if t == 3:
                            ys[p + 1, 0, pl.ds(j, 1), :] = total[7:8, :]
                        if t == 0:
                            ys[p + 1, 1, pl.ds(j, 1), :] = total[0:1, :]
                        pack(total, j, t, held)
            if x == 4 and not last:
                begin(x_copies(p + 1))
        if not last:
            for h in range(2):
                zs[p + 1, pl.ds(8 * h, 8), :] = held[h]
            begin(yz_copies(p + 1))

    interior(0)
    loads[5].wait()
    finish(0, first=True)

    def power(p, carry):
        interior(p)
        products(p)
        finish(p)
        return carry

    lax.fori_loop(1, 4, power, 0)
    interior(4)
    products(4)
    finish(4, last=True)
    products(5)

    def everyone(row, offsets, rows_ref, mine, count, slot, meanwhile):
        msg[slot, :, :] = row
        copies = [
            pltpu.make_async_remote_copy(
                msg.at[slot, pl.ds(0, 1), :], rows_ref.at[pl.ds(mine, 1), :], asem.at[slot, 0], asem.at[slot, 1],
                device_id=shifted(o), device_id_type=MESH) for o in offsets
        ]
        begin(copies)
        meanwhile()
        others = rows_ref.at[pl.ds(0, count - 1), :]
        pltpu.make_async_copy(others, others, asem.at[slot, 1]).wait()
        total = None
        for r in range(count // 8):
            part = jnp.where(sub + 8 * r == mine, row, rows_ref[pl.ds(8 * r, 8), :])
            total = part if total is None else total + part
        return jnp.broadcast_to(jnp.sum(total, axis=0, keepdims=True), (8, 128))

    def sent(rows_ref, count, slot):
        others = rows_ref.at[pl.ds(0, count - 1), :]
        pltpu.make_async_copy(others, others, asem.at[slot, 0]).wait()

    g = jnp.broadcast_to(jnp.sum(G[...], axis=0, keepdims=True), (8, 128))
    def faces_sent():
        for p in range(5):
            all_six(p, ssem)
        c_copy.wait_send()

    g = everyone(g, plane, row_a, me[1] * nz + me[2], ny * nz, 0, faces_sent)
    g = everyone(g, line, row_b, me[0], nx, 1, lambda: sent(row_a, ny * nz, 0))

    ahead, after = rolled(g, -10), rolled(g, -20)
    normal = (SHIFT * SHIFT) * g + (2 * SHIFT * SCALE) * ahead + (SCALE * SCALE) * after
    right = SHIFT * g + SCALE * ahead
    entries = jnp.where(lane < 80, normal, rolled(right, 70))
    spread = jnp.concatenate([jnp.where(sub + 8 * r == lane, entries, 0.0) for r in range(16)], axis=0)
    rep[...] = lane_sums(spread)

    def entry(r):
        return jnp.broadcast_to(rep[pl.ds(r, 1), :], (8, 128))

    n = 16
    a = {}
    for i in range(n):
        for j in range(i + 1):
            a[i, j] = entry(10 * (i // 4 + j // 4 + 1) + PLACE[i % 4, j % 4])
    b = []
    for i in range(n):
        value = entry(80 + 10 * (i // 4) + PLACE[i % 4, 3])
        for j in range(3):
            value = jnp.where(sub == j, entry(80 + 10 * (i // 4) + PLACE[i % 4, j]), value)
        b.append(value)
    inverse = []
    for k in range(n):
        inverse.append(1.0 / a[k, k])
        for i in range(k + 1, n):
            factor = a[i, k] * inverse[k]
            for j in range(k + 1, i + 1):
                a[i, j] = a[i, j] - factor * a[j, k]
            b[i] = b[i] - factor * b[k]
    for i in reversed(range(n)):
        b[i] = b[i] * inverse[i]
        W[i, :, :] = b[i]
        for j in range(i):
            b[j] = b[j] - a[i, j] * b[i]

    def update(x, carry):
        total = [[V[0, x, f, pl.ds(TOP + 8 * t, 8), :] for t in range(4)] for f in range(4)]
        for c in range(16):
            v = [V[1 + c // 4, x, c % 4, pl.ds(TOP + 8 * t, 8), :] for t in range(4)]
            for f in range(4):
                w = jnp.broadcast_to(W[c, pl.ds(f, 1), :], (8, 128))
                for t in range(4):
                    total[f][t] = total[f][t] + w * v[t]
        for f in range(4):
            for t in range(4):
                out[f, x, pl.ds(8 * t, 8), :] = total[f][t]
        return carry

    lax.fori_loop(0, 5, update, 0)

    sent(row_b, nx, 1)


def solution(mesh):
    sizes = tuple(mesh.shape[axis] for axis in AXES)
    spec = P(None, "gx", "gy", "gz")

    def local(start, rhs_block, coefficients):
        vmem = lambda *shape: pltpu.VMEM(shape, F32)
        return pl.pallas_call(
            lambda *refs: kernel(sizes, *refs),
            out_shape=jax.ShapeDtypeStruct(start.shape, F32),
            in_specs=[pl.BlockSpec(memory_space=pl.ANY)] * 3,
            out_specs=pl.BlockSpec(memory_space=pltpu.VMEM),
            scratch_shapes=[
                vmem(6, 5, 4, 48, 128), vmem(4, 5, 32, 128), vmem(4, 5, 32, 128),
                vmem(5, 32, 128), vmem(5, 32, 128), vmem(5, 48, 128),
                vmem(5, 32, 128), vmem(5, 32, 128), vmem(5, 32, 128),
                vmem(2, 32, 128), vmem(2, 5, 8, 128),
                vmem(5, 11, 32, 128), vmem(32, 128),
                vmem(5, 2, 32, 128), vmem(5, 16, 128),
                vmem(8, 128), vmem(192, 128), vmem(32, 128), vmem(16, 128), vmem(2, 8, 128), vmem(128, 128), vmem(16, 8, 128),
                pltpu.SemaphoreType.DMA((6,)), pltpu.SemaphoreType.DMA((6,)),
                pltpu.SemaphoreType.DMA((6,)), pltpu.SemaphoreType.DMA((2, 2)),
            ],
            compiler_params=pltpu.CompilerParams(
                collective_id=0, has_side_effects=True, vmem_limit_bytes=54764 << 10
            ),
        )(start, rhs_block, coefficients)

    return jax.shard_map(local, mesh=mesh, in_specs=(spec,) * 3, out_specs=spec, check_vma=False)
```

```python
import itertools

import jax
import jax.numpy as jnp
from jax import lax
from jax.experimental import pallas as pl
from jax.experimental.pallas import tpu as pltpu
from jax.sharding import PartitionSpec as P

MESH = pl.DeviceIdType.MESH
F32 = jnp.float32
AXES = ("gx", "gy", "gz")
SHIFT, SCALE = 8.75, 4.0
PAIRS = [(i, j) for i in range(4) for j in range(i, 4)]
PLACE = {(i, j): PAIRS.index((min(i, j), max(i, j))) for i in range(4) for j in range(4)}
TOP = 8
XLO, XHI, YLO, YHI, ZLO, ZHI = range(6)
YF, ZF = 8, 10


def rolled(tile, shift):
    return pltpu.roll(tile, shift % 128, 1)


def lane_sums(x):
    high = x.astype(jnp.bfloat16)
    rest = x - high.astype(F32)
    middle = rest.astype(jnp.bfloat16)
    low = (rest - middle.astype(F32)).astype(jnp.bfloat16)
    terms = jnp.concatenate([low, middle, high], axis=1)
    return jnp.dot(terms, jnp.ones((384, 128), jnp.bfloat16), preferred_element_type=F32)


def kernel(
    sizes, start, rhs, coef, out,
    V, rhs_v, coef_v, bd, bc1, bc2, bc3p, bc3m, e3, e1, e2,
    faces, c1h, ys, zs, G, parts, row_a, row_b, msg, W,
    lsem, ssem, rsem, asem,
):
    nx, ny, nz = sizes
    me = [lax.axis_index(axis) for axis in AXES]

    def ahead_by(axis, d):
        place = me[axis] + d
        return place if d == 0 else jnp.where(place >= sizes[axis], place - sizes[axis], place)

    places = [[ahead_by(axis, d) for d in range(sizes[axis])] for axis in range(3)]

    def shifted(offset):
        return tuple(places[axis][d % sizes[axis]] for axis, d in enumerate(offset))

    neighbours = [shifted(o) for o in ((1, 0, 0), (-1, 0, 0), (0, 1, 0), (0, -1, 0), (0, 0, 1), (0, 0, -1))]

    def far(o):
        return -sum(min(d, s - d) for d, s in zip(o, sizes))

    plane = sorted([(0, b, c) for b, c in itertools.product(range(ny), range(nz)) if b or c], key=far)
    line = sorted([(a, 0, 0) for a in range(1, nx)], key=far)

    barrier = pltpu.get_barrier_semaphore()
    twin = me[0] + 1 - 2 * lax.rem(me[0], 2)
    near = neighbours[2:] + [
        (jnp.where(base + d >= nx, base + d - nx, base + d), me[1], me[2])
        for base in (twin, me[0]) for d in (2, nx - 2)
    ] + [(twin, me[1], me[2])]
    for partner in near:
        pl.semaphore_signal(barrier, inc=1, device_id=partner, device_id_type=MESH)

    loads = [
        pltpu.make_async_copy(start.at[f], V.at[0, :, f, pl.ds(TOP, 32), :], lsem.at[f]) for f in range(4)
    ] + [pltpu.make_async_copy(coef, coef_v, lsem.at[4]), pltpu.make_async_copy(rhs, rhs_v, lsem.at[5])]
    for copy in loads:
        copy.start()

    lane = lax.broadcasted_iota(jnp.int32, (8, 128), 1)
    sub = lax.broadcasted_iota(jnp.int32, (8, 128), 0)
    pair_lane = lax.shift_right_logical(lane, 1)
    even_lane = lax.rem(lane, 2) == 0
    zero = jnp.zeros((8, 128), F32)

    def inside(axis, edge):
        return jnp.where(me[axis] == edge, 0.0, 1.0).astype(F32)

    low = [inside(0, 0), inside(1, 0), inside(2, 0)]
    high = [inside(0, nx - 1), inside(1, ny - 1), inside(2, nz - 1)]

    def send(source, target, p, way):
        return pltpu.make_async_remote_copy(
            source, target, ssem.at[p], rsem.at[p], device_id=neighbours[way], device_id_type=MESH
        )

    def x_copies(p):
        return [
            send(V.at[p, 4 - 4 * d, :, pl.ds(TOP, 32), :], faces.at[p, pl.ds(4 * d, 4)], p, XLO + d) for d in range(2)
        ]

    def yz_copies(p):
        return [send(ys.at[p, d], faces.at[p, YF + d], p, YLO + d) for d in range(2)] + [
            send(zs.at[p], faces.at[p, ZF, pl.ds(16 * d, 16), :], p, ZLO + d) for d in range(2)
        ]

    def all_six(p, sem):
        pltpu.make_async_copy(faces.at[p], faces.at[p], sem.at[p]).wait()

    c_copy = pltpu.make_async_remote_copy(
        coef_v.at[1, 4], c1h, ssem.at[5], rsem.at[5], device_id=neighbours[0], device_id_type=MESH
    )

    def begin(copies):
        for copy in copies:
            copy.start()

    def pack(tile, spot, t, held):
        k = 2 * spot + t % 2
        held[t // 2] = jnp.where(pair_lane == k, rolled(tile, 2 * k + 1), held[t // 2])

    for copy in loads[:5]:
        copy.wait()
    held = [zero, zero]
    for x in range(5):
        for f in range(4):
            j = 4 * x + f
            ys[0, 0, pl.ds(j, 1), :] = V[0, x, f, pl.ds(TOP + 31, 1), :]
            ys[0, 1, pl.ds(j, 1), :] = V[0, x, f, pl.ds(TOP, 1), :]
            for t in range(4):
                pack(V[0, x, f, pl.ds(TOP + 8 * t, 8), :], j, t, held)
        ys[0, 0, pl.ds(20 + x, 1), :] = coef_v[2, x, pl.ds(31, 1), :]
        ys[0, 1, pl.ds(20 + x, 1), :] = coef_v[2, x, pl.ds(31, 1), :]
        for t in range(4):
            pack(coef_v[3, x, pl.ds(8 * t, 8), :], 20 + x, t, held)
    for h in range(2):
        zs[0, pl.ds(8 * h, 8), :] = held[h]

    pl.semaphore_wait(barrier, len(near))
    begin(yz_copies(0) + x_copies(0) + [c_copy])

    def clear(i, carry):
        for f in range(4):
            for x in range(5):
                V[i, x, f, pl.ds(0, 8), :] = zero
                V[i, x, f, pl.ds(TOP + 32, 8), :] = zero
        return carry

    lax.fori_loop(0, 5, clear, 0)
    for x in range(5):
        bc2[x, pl.ds(0, 8), :] = zero
    G[...] = zero
    parts[pl.ds(160, 32), :] = jnp.zeros((32, 128), F32)

    for x in range(5):
        for t in range(4):
            rows = pl.ds(8 * t, 8)
            bc2[x, pl.ds(TOP + 8 * t, 8), :] = -0.25 * coef_v[2, x, rows, :]
        for t in range(4):
            rows = pl.ds(8 * t, 8)
            n1 = -0.25 * coef_v[1, x, rows, :]
            n3 = -0.25 * coef_v[3, x, rows, :]
            bc1[x, rows, :] = n1
            bc3p[x, rows, :] = jnp.where(lane == 127, 0.0, n3)
            back = jnp.where(lane == 0, 0.0, rolled(n3, 1))
            bc3m[x, rows, :] = back
            e3[x, rows, :] = jnp.where(lane == 127, n3 * high[2], 0.0)
            total = n1 + n3 + back + bc2[x, pl.ds(TOP + 8 * t, 8), :] + bc2[x, pl.ds(TOP - 1 + 8 * t, 8), :]
            if x > 0:
                total = total + bc1[x - 1, rows, :]
            bd[x, rows, :] = 0.25 * (coef_v[0, x, rows, :] - SHIFT) - total
            if x == 4:
                e1[1, rows, :] = n1 * high[0]
        e2[1, x, :, :] = jnp.where(sub == 7, bc2[x, pl.ds(TOP + 24, 8), :] * high[1], 0.0)

    def interior(p, first=False):
        def layer(x, below, above):
            for t in range(4):
                rows = pl.ds(8 * t, 8)
                c_d, c_xp = bd[x, rows, :], bc1[x, rows, :]
                c_yp, c_ym = bc2[x, pl.ds(TOP + 8 * t, 8), :], bc2[x, pl.ds(TOP - 1 + 8 * t, 8), :]
                c_zp, c_zm = bc3p[x, rows, :], bc3m[x, rows, :]
                for f in range(4):
                    v = V[p, x, f, pl.ds(TOP + 8 * t, 8), :]
                    total = c_d * v
                    total = total + c_yp * V[p, x, f, pl.ds(TOP + 1 + 8 * t, 8), :]
                    total = total + c_ym * V[p, x, f, pl.ds(TOP - 1 + 8 * t, 8), :]
                    if above:
                        total = total + c_xp * V[p, x + 1, f, pl.ds(TOP + 8 * t, 8), :]
                    if below:
                        total = total + bc1[x - 1, rows, :] * V[p, x - 1, f, pl.ds(TOP + 8 * t, 8), :]
                    total = total + c_zp * rolled(v, -1)
                    total = total + c_zm * rolled(v, 1)
                    if first:
                        total = rhs_v[f, x, rows, :] - SHIFT * v - SCALE * total
                    V[p + 1, x, f, pl.ds(TOP + 8 * t, 8), :] = total

        layer(0, False, True)

        def middle(x, carry):
            layer(x, True, True)
            return carry

        lax.fori_loop(1, 4, middle, 0)
        layer(4, True, False)

    def products(p):
        def layer(x, sums):
            sums = list(sums)
            for t in range(4):
                new = [V[p, x, f, pl.ds(TOP + 8 * t, 8), :] for f in range(4)]
                old = [V[p - 1, x, f, pl.ds(TOP + 8 * t, 8), :] for f in range(4)]
                for q, (i, j) in enumerate(PAIRS):
                    sums[q] = sums[q] + old[i] * new[j]
                    sums[10 + q] = sums[10 + q] + new[i] * new[j]
            return tuple(sums)

        sums = lax.fori_loop(0, 5, layer, (zero,) * 20)
        for q in range(20):
            parts[pl.ds(8 * q, 8), :] = sums[q]
        rows = parts[pl.ds(0, 24, stride=8), :]
        for r in range(1, 8):
            rows = rows + parts[pl.ds(r, 24, stride=8), :]
        totals = lane_sums(rows)
        block = G[...]
        for h in range(3):
            mine = lane == sub + (20 * p - 20 + 8 * h)
            if h == 2:
                mine = mine & (sub < 4)
            block = block + jnp.where(mine, totals[8 * h : 8 * h + 8, :], 0.0)
        G[...] = block

    def finish(p, first=False, last=False):
        all_six(p, rsem)
        if first:
            c_copy.wait_recv()
        both = [
            jnp.where(even_lane, faces[p, ZF, pl.ds(8 * h, 8), :], rolled(faces[p, ZF, pl.ds(16 + 8 * h, 8), :], -2))
            for h in range(2)
        ]
        held = [zero, zero]
        for x in (0, 4, 1, 2, 3):
            for t in range(4):
                rows = pl.ds(8 * t, 8)
                edge = e3[x, rows, :]
                if first:
                    k = 2 * (20 + x) + t % 2
                    more = jnp.where(lane == 0, (-0.25 * low[2]) * rolled(both[t // 2], -2 * k), 0.0)
                    edge = edge + more
                    e3[x, rows, :] = edge
                    if x == 0:
                        face = (-0.25 * low[0]) * c1h[rows, :]
                        e1[0, rows, :] = face
                        more = more + face
                    if t == 0:
                        row = jnp.broadcast_to(faces[p, YF, pl.ds(20 + x, 1), :], (8, 128))
                        face = jnp.where(sub == 0, (-0.25 * low[1]) * row, 0.0)
                        e2[0, x, :, :] = face
                        more = more + face
                    bd[x, rows, :] = bd[x, rows, :] - more
                for f in range(4):
                    j = 4 * x + f
                    k = 2 * j + t % 2
                    cells = pl.ds(TOP + 8 * t, 8)
                    total = -more * V[p, x, f, cells, :] if first else V[p + 1, x, f, cells, :]
                    if x == 0:
                        total = total + e1[0, rows, :] * faces[p, f, rows, :]
                    if x == 4:
                        total = total + e1[1, rows, :] * faces[p, 4 + f, rows, :]
                    if t == 0:
                        total = total + e2[0, x, :, :] * jnp.broadcast_to(faces[p, YF, pl.ds(j, 1), :], (8, 128))
                    if t == 3:
                        total = total + e2[1, x, :, :] * jnp.broadcast_to(faces[p, YF + 1, pl.ds(j, 1), :], (8, 128))
                    total = total + edge * rolled(both[t // 2], -2 * k)
                    if first:
                        total = V[p + 1, x, f, cells, :] - SCALE * total
                    V[p + 1, x, f, cells, :] = total
                    if not last:
                        if t == 3:
                            ys[p + 1, 0, pl.ds(j, 1), :] = total[7:8, :]
                        if t == 0:
                            ys[p + 1, 1, pl.ds(j, 1), :] = total[0:1, :]
                        pack(total, j, t, held)
            if x == 4 and not last:
                begin(x_copies(p + 1))
        if not last:
            for h in range(2):
                zs[p + 1, pl.ds(8 * h, 8), :] = held[h]
            begin(yz_copies(p + 1))

    loads[5].wait()
    interior(0, first=True)
    finish(0, first=True)

    def power(p, carry):
        interior(p)
        products(p)
        finish(p)
        return carry

    lax.fori_loop(1, 4, power, 0)
    interior(4)
    products(4)
    finish(4, last=True)
    products(5)

    def everyone(row, offsets, rows_ref, mine, count, slot, meanwhile):
        msg[slot, :, :] = row
        copies = [
            pltpu.make_async_remote_copy(
                msg.at[slot, pl.ds(0, 1), :], rows_ref.at[pl.ds(mine, 1), :], asem.at[slot, 0], asem.at[slot, 1],
                device_id=shifted(o), device_id_type=MESH) for o in offsets
        ]
        begin(copies)
        meanwhile()
        others = rows_ref.at[pl.ds(0, count - 1), :]
        pltpu.make_async_copy(others, others, asem.at[slot, 1]).wait()
        total = None
        for r in range(count // 8):
            part = jnp.where(sub + 8 * r == mine, row, rows_ref[pl.ds(8 * r, 8), :])
            total = part if total is None else total + part
        return jnp.broadcast_to(jnp.sum(total, axis=0, keepdims=True), (8, 128))

    def sent(rows_ref, count, slot):
        others = rows_ref.at[pl.ds(0, count - 1), :]
        pltpu.make_async_copy(others, others, asem.at[slot, 0]).wait()

    g = jnp.broadcast_to(jnp.sum(G[...], axis=0, keepdims=True), (8, 128))
    def faces_sent():
        for p in range(5):
            all_six(p, ssem)
        c_copy.wait_send()

    g = everyone(g, line, row_b, me[0], nx, 1, faces_sent)
    g = everyone(g, plane, row_a, me[1] * nz + me[2], ny * nz, 0, lambda: sent(row_b, nx, 1))

    ahead, after = rolled(g, -10), rolled(g, -20)
    normal = (SHIFT * SHIFT) * g + (2 * SHIFT * SCALE) * ahead + (SCALE * SCALE) * after
    right = SHIFT * g + SCALE * ahead
    entries = jnp.where(lane < 80, normal, rolled(right, 70))
    def entry(r):
        return jnp.broadcast_to(entries[:, r : r + 1], (8, 128))

    n = 16
    a = {}
    for i in range(n):
        for j in range(i + 1):
            a[i, j] = entry(10 * (i // 4 + j // 4 + 1) + PLACE[i % 4, j % 4])
    b = []
    for i in range(n):
        value = entry(80 + 10 * (i // 4) + PLACE[i % 4, 3])
        for j in range(3):
            value = jnp.where(sub == j, entry(80 + 10 * (i // 4) + PLACE[i % 4, j]), value)
        b.append(value)
    inverse = []
    for k in range(n):
        inverse.append(1.0 / a[k, k])
        for i in range(k + 1, n):
            factor = a[i, k] * inverse[k]
            for j in range(k + 1, i + 1):
                a[i, j] = a[i, j] - factor * a[j, k]
            b[i] = b[i] - factor * b[k]
    for i in reversed(range(n)):
        b[i] = b[i] * inverse[i]
        W[i, :, :] = b[i]
        for j in range(i):
            b[j] = b[j] - a[i, j] * b[i]

    def update(x, carry):
        total = [[V[0, x, f, pl.ds(TOP + 8 * t, 8), :] for t in range(4)] for f in range(4)]
        for c in range(16):
            v = [V[1 + c // 4, x, c % 4, pl.ds(TOP + 8 * t, 8), :] for t in range(4)]
            for f in range(4):
                w = jnp.broadcast_to(W[c, pl.ds(f, 1), :], (8, 128))
                for t in range(4):
                    total[f][t] = total[f][t] + w * v[t]
        for f in range(4):
            for t in range(4):
                out[f, x, pl.ds(8 * t, 8), :] = total[f][t]
        return carry

    lax.fori_loop(0, 5, update, 0)

    sent(row_a, ny * nz, 0)


def solution(mesh):
    sizes = tuple(mesh.shape[axis] for axis in AXES)
    spec = P(None, "gx", "gy", "gz")

    def local(start, rhs_block, coefficients):
        vmem = lambda *shape: pltpu.VMEM(shape, F32)
        return pl.pallas_call(
            lambda *refs: kernel(sizes, *refs),
            out_shape=jax.ShapeDtypeStruct(start.shape, F32),
            in_specs=[pl.BlockSpec(memory_space=pl.ANY)] * 3,
            out_specs=pl.BlockSpec(memory_space=pltpu.VMEM),
            scratch_shapes=[
                vmem(6, 5, 4, 48, 128), vmem(4, 5, 32, 128), vmem(4, 5, 32, 128),
                vmem(5, 32, 128), vmem(5, 32, 128), vmem(5, 48, 128),
                vmem(5, 32, 128), vmem(5, 32, 128), vmem(5, 32, 128),
                vmem(2, 32, 128), vmem(2, 5, 8, 128),
                vmem(5, 11, 32, 128), vmem(32, 128),
                vmem(5, 2, 32, 128), vmem(5, 16, 128),
                vmem(8, 128), vmem(192, 128), vmem(32, 128), vmem(16, 128), vmem(2, 8, 128), vmem(16, 8, 128),
                pltpu.SemaphoreType.DMA((6,)), pltpu.SemaphoreType.DMA((6,)),
                pltpu.SemaphoreType.DMA((6,)), pltpu.SemaphoreType.DMA((2, 2)),
            ],
            compiler_params=pltpu.CompilerParams(
                collective_id=0, has_side_effects=True, vmem_limit_bytes=54764 << 10
            ),
        )(start, rhs_block, coefficients)

    return jax.shard_map(local, mesh=mesh, in_specs=(spec,) * 3, out_specs=spec, check_vma=False)
```

```python
import itertools

import jax
import jax.numpy as jnp
from jax import lax
from jax.experimental import pallas as pl
from jax.experimental.pallas import tpu as pltpu
from jax.sharding import PartitionSpec as P

MESH = pl.DeviceIdType.MESH
F32 = jnp.float32
AXES = ("gx", "gy", "gz")
SHIFT, SCALE = 8.75, 4.0
PAIRS = [(i, j) for i in range(4) for j in range(i, 4)]
PLACE = {(i, j): PAIRS.index((min(i, j), max(i, j))) for i in range(4) for j in range(4)}
TOP = 8
XLO, XHI, YLO, YHI, ZLO, ZHI = range(6)
YF, ZF = 8, 10


def rolled(tile, shift):
    return pltpu.roll(tile, shift % 128, 1)


def lane_sums(x):
    high = x.astype(jnp.bfloat16)
    rest = x - high.astype(F32)
    middle = rest.astype(jnp.bfloat16)
    low = (rest - middle.astype(F32)).astype(jnp.bfloat16)
    terms = jnp.concatenate([low, middle, high], axis=1)
    return jnp.dot(terms, jnp.ones((384, 128), jnp.bfloat16), preferred_element_type=F32)


def kernel(
    sizes, start, rhs, coef, out,
    V, rhs_v, coef_v, bd, bc1, bc2, bc3p, bc3m, e3, e1, e2,
    faces, c1h, ys, zs, G, parts, row_a, row_b, msg, W,
    lsem, ssem, rsem, asem,
):
    nx, ny, nz = sizes
    me = [lax.axis_index(axis) for axis in AXES]

    def ahead_by(axis, d):
        place = me[axis] + d
        return place if d == 0 else jnp.where(place >= sizes[axis], place - sizes[axis], place)

    places = [[ahead_by(axis, d) for d in range(sizes[axis])] for axis in range(3)]

    def shifted(offset):
        return tuple(places[axis][d % sizes[axis]] for axis, d in enumerate(offset))

    neighbours = [shifted(o) for o in ((1, 0, 0), (-1, 0, 0), (0, 1, 0), (0, -1, 0), (0, 0, 1), (0, 0, -1))]

    def far(o):
        return -sum(min(d, s - d) for d, s in zip(o, sizes))

    plane = sorted([(0, b, c) for b, c in itertools.product(range(ny), range(nz)) if b or c], key=far)
    line = sorted([(a, 0, 0) for a in range(1, nx)], key=far)

    barrier = pltpu.get_barrier_semaphore()
    twin = me[0] + 1 - 2 * lax.rem(me[0], 2)
    near = neighbours[2:] + [
        (jnp.where(base + d >= nx, base + d - nx, base + d), me[1], me[2])
        for base in (twin, me[0]) for d in (2, nx - 2)
    ] + [(twin, me[1], me[2])]
    for partner in near:
        pl.semaphore_signal(barrier, inc=1, device_id=partner, device_id_type=MESH)

    loads = [
        pltpu.make_async_copy(start.at[f], V.at[0, :, f, pl.ds(TOP, 32), :], lsem.at[f]) for f in range(4)
    ] + [pltpu.make_async_copy(coef, coef_v, lsem.at[4]), pltpu.make_async_copy(rhs, rhs_v, lsem.at[5])]
    for copy in loads:
        copy.start()

    lane = lax.broadcasted_iota(jnp.int32, (8, 128), 1)
    sub = lax.broadcasted_iota(jnp.int32, (8, 128), 0)
    pair_lane = lax.shift_right_logical(lane, 1)
    even_lane = lax.rem(lane, 2) == 0
    zero = jnp.zeros((8, 128), F32)

    def inside(axis, edge):
        return jnp.where(me[axis] == edge, 0.0, 1.0).astype(F32)

    low = [inside(0, 0), inside(1, 0), inside(2, 0)]
    high = [inside(0, nx - 1), inside(1, ny - 1), inside(2, nz - 1)]

    def send(source, target, p, way):
        return pltpu.make_async_remote_copy(
            source, target, ssem.at[p], rsem.at[p], device_id=neighbours[way], device_id_type=MESH
        )

    def x_copies(p):
        return [
            send(V.at[p, 4 - 4 * d, :, pl.ds(TOP, 32), :], faces.at[p, pl.ds(4 * d, 4)], p, XLO + d) for d in range(2)
        ]

    def yz_copies(p):
        return [send(ys.at[p, d], faces.at[p, YF + d], p, YLO + d) for d in range(2)] + [
            send(zs.at[p], faces.at[p, ZF, pl.ds(16 * d, 16), :], p, ZLO + d) for d in range(2)
        ]

    def all_six(p, sem):
        pltpu.make_async_copy(faces.at[p], faces.at[p], sem.at[p]).wait()

    c_copy = pltpu.make_async_remote_copy(
        coef_v.at[1, 4], c1h, ssem.at[5], rsem.at[5], device_id=neighbours[0], device_id_type=MESH
    )

    def begin(copies):
        for copy in copies:
            copy.start()

    def pack(tile, spot, t, held):
        k = 2 * spot + t % 2
        held[t // 2] = jnp.where(pair_lane == k, rolled(tile, 2 * k + 1), held[t // 2])

    for copy in loads[:5]:
        copy.wait()
    held = [zero, zero]
    for x in range(5):
        for f in range(4):
            j = 4 * x + f
            ys[0, 0, pl.ds(j, 1), :] = V[0, x, f, pl.ds(TOP + 31, 1), :]
            ys[0, 1, pl.ds(j, 1), :] = V[0, x, f, pl.ds(TOP, 1), :]
            for t in range(4):
                pack(V[0, x, f, pl.ds(TOP + 8 * t, 8), :], j, t, held)
        ys[0, 0, pl.ds(20 + x, 1), :] = coef_v[2, x, pl.ds(31, 1), :]
        ys[0, 1, pl.ds(20 + x, 1), :] = coef_v[2, x, pl.ds(31, 1), :]
        for t in range(4):
            pack(coef_v[3, x, pl.ds(8 * t, 8), :], 20 + x, t, held)
    for h in range(2):
        zs[0, pl.ds(8 * h, 8), :] = held[h]

    pl.semaphore_wait(barrier, len(near))
    begin(yz_copies(0) + x_copies(0) + [c_copy])

    def clear(i, carry):
        for f in range(4):
            for x in range(5):
                V[i, x, f, pl.ds(0, 8), :] = zero
                V[i, x, f, pl.ds(TOP + 32, 8), :] = zero
        return carry

    lax.fori_loop(0, 5, clear, 0)
    for x in range(5):
        bc2[x, pl.ds(0, 8), :] = zero
    G[...] = zero
    parts[pl.ds(160, 32), :] = jnp.zeros((32, 128), F32)

    for x in range(5):
        for t in range(4):
            rows = pl.ds(8 * t, 8)
            bc2[x, pl.ds(TOP + 8 * t, 8), :] = -0.25 * coef_v[2, x, rows, :]
        for t in range(4):
            rows = pl.ds(8 * t, 8)
            n1 = -0.25 * coef_v[1, x, rows, :]
            n3 = -0.25 * coef_v[3, x, rows, :]
            bc1[x, rows, :] = n1
            bc3p[x, rows, :] = jnp.where(lane == 127, 0.0, n3)
            back = jnp.where(lane == 0, 0.0, rolled(n3, 1))
            bc3m[x, rows, :] = back
            e3[x, rows, :] = jnp.where(lane == 127, n3 * high[2], 0.0)
            total = n1 + n3 + back + bc2[x, pl.ds(TOP + 8 * t, 8), :] + bc2[x, pl.ds(TOP - 1 + 8 * t, 8), :]
            if x > 0:
                total = total + bc1[x - 1, rows, :]
            bd[x, rows, :] = 0.25 * (coef_v[0, x, rows, :] - SHIFT) - total
            if x == 4:
                e1[1, rows, :] = n1 * high[0]
        e2[1, x, :, :] = jnp.where(sub == 7, bc2[x, pl.ds(TOP + 24, 8), :] * high[1], 0.0)

    def interior(p, first=False):
        def layer(x, below, above):
            for t in range(4):
                rows = pl.ds(8 * t, 8)
                c_d, c_xp = bd[x, rows, :], bc1[x, rows, :]
                c_yp, c_ym = bc2[x, pl.ds(TOP + 8 * t, 8), :], bc2[x, pl.ds(TOP - 1 + 8 * t, 8), :]
                c_zp, c_zm = bc3p[x, rows, :], bc3m[x, rows, :]
                for f in range(4):
                    v = V[p, x, f, pl.ds(TOP + 8 * t, 8), :]
                    total = c_d * v
                    total = total + c_yp * V[p, x, f, pl.ds(TOP + 1 + 8 * t, 8), :]
                    total = total + c_ym * V[p, x, f, pl.ds(TOP - 1 + 8 * t, 8), :]
                    if above:
                        total = total + c_xp * V[p, x + 1, f, pl.ds(TOP + 8 * t, 8), :]
                    if below:
                        total = total + bc1[x - 1, rows, :] * V[p, x - 1, f, pl.ds(TOP + 8 * t, 8), :]
                    total = total + c_zp * rolled(v, -1)
                    total = total + c_zm * rolled(v, 1)
                    if first:
                        total = rhs_v[f, x, rows, :] - SHIFT * v - SCALE * total
                    V[p + 1, x, f, pl.ds(TOP + 8 * t, 8), :] = total

        layer(0, False, True)

        def middle(x, carry):
            layer(x, True, True)
            return carry

        lax.fori_loop(1, 4, middle, 0)
        layer(4, True, False)

    def products(p):
        def layer(x, sums):
            sums = list(sums)
            for t in range(4):
                new = [V[p, x, f, pl.ds(TOP + 8 * t, 8), :] for f in range(4)]
                old = [V[p - 1, x, f, pl.ds(TOP + 8 * t, 8), :] for f in range(4)]
                for q, (i, j) in enumerate(PAIRS):
                    sums[q] = sums[q] + old[i] * new[j]
                    sums[10 + q] = sums[10 + q] + new[i] * new[j]
            return tuple(sums)

        sums = lax.fori_loop(0, 5, layer, (zero,) * 20)
        for q in range(20):
            parts[pl.ds(8 * q, 8), :] = sums[q]
        rows = parts[pl.ds(0, 24, stride=8), :]
        for r in range(1, 8):
            rows = rows + parts[pl.ds(r, 24, stride=8), :]
        totals = lane_sums(rows)
        block = G[...]
        for h in range(3):
            mine = lane == sub + (20 * p - 20 + 8 * h)
            if h == 2:
                mine = mine & (sub < 4)
            block = block + jnp.where(mine, totals[8 * h : 8 * h + 8, :], 0.0)
        G[...] = block

    def finish(p, first=False, last=False):
        all_six(p, rsem)
        if first:
            c_copy.wait_recv()
        both = [
            jnp.where(even_lane, faces[p, ZF, pl.ds(8 * h, 8), :], rolled(faces[p, ZF, pl.ds(16 + 8 * h, 8), :], -2))
            for h in range(2)
        ]
        held = [zero, zero]
        for x in (0, 4, 1, 2, 3):
            for t in range(4):
                rows = pl.ds(8 * t, 8)
                edge = e3[x, rows, :]
                if first:
                    k = 2 * (20 + x) + t % 2
                    more = jnp.where(lane == 0, (-0.25 * low[2]) * rolled(both[t // 2], -2 * k), 0.0)
                    edge = edge + more
                    e3[x, rows, :] = edge
                    if x == 0:
                        face = (-0.25 * low[0]) * c1h[rows, :]
                        e1[0, rows, :] = face
                        more = more + face
                    if t == 0:
                        row = jnp.broadcast_to(faces[p, YF, pl.ds(20 + x, 1), :], (8, 128))
                        face = jnp.where(sub == 0, (-0.25 * low[1]) * row, 0.0)
                        e2[0, x, :, :] = face
                        more = more + face
                    bd[x, rows, :] = bd[x, rows, :] - more
                for f in range(4):
                    j = 4 * x + f
                    k = 2 * j + t % 2
                    cells = pl.ds(TOP + 8 * t, 8)
                    total = -more * V[p, x, f, cells, :] if first else V[p + 1, x, f, cells, :]
                    if x == 0:
                        total = total + e1[0, rows, :] * faces[p, f, rows, :]
                    if x == 4:
                        total = total + e1[1, rows, :] * faces[p, 4 + f, rows, :]
                    if t == 0:
                        total = total + e2[0, x, :, :] * jnp.broadcast_to(faces[p, YF, pl.ds(j, 1), :], (8, 128))
                    if t == 3:
                        total = total + e2[1, x, :, :] * jnp.broadcast_to(faces[p, YF + 1, pl.ds(j, 1), :], (8, 128))
                    total = total + edge * rolled(both[t // 2], -2 * k)
                    if first:
                        total = V[p + 1, x, f, cells, :] - SCALE * total
                    V[p + 1, x, f, cells, :] = total
                    if not last:
                        if t == 3:
                            ys[p + 1, 0, pl.ds(j, 1), :] = total[7:8, :]
                        if t == 0:
                            ys[p + 1, 1, pl.ds(j, 1), :] = total[0:1, :]
                        pack(total, j, t, held)
            if x in (0, 4) and not last:
                begin([x_copies(p + 1)[1 - x // 4]])
        if not last:
            for h in range(2):
                zs[p + 1, pl.ds(8 * h, 8), :] = held[h]
            begin(yz_copies(p + 1))

    loads[5].wait()
    interior(0, first=True)
    finish(0, first=True)

    def power(p, carry):
        interior(p)
        products(p)
        finish(p)
        return carry

    lax.fori_loop(1, 4, power, 0)
    interior(4)
    products(4)
    finish(4, last=True)
    products(5)

    def everyone(row, offsets, rows_ref, mine, count, slot, meanwhile):
        msg[slot, :, :] = row
        copies = [
            pltpu.make_async_remote_copy(
                msg.at[slot, pl.ds(0, 1), :], rows_ref.at[pl.ds(mine, 1), :], asem.at[slot, 0], asem.at[slot, 1],
                device_id=shifted(o), device_id_type=MESH) for o in offsets
        ]
        begin(copies)
        meanwhile()
        others = rows_ref.at[pl.ds(0, count - 1), :]
        pltpu.make_async_copy(others, others, asem.at[slot, 1]).wait()
        total = None
        for r in range(count // 8):
            part = jnp.where(sub + 8 * r == mine, row, rows_ref[pl.ds(8 * r, 8), :])
            total = part if total is None else total + part
        return jnp.broadcast_to(jnp.sum(total, axis=0, keepdims=True), (8, 128))

    def sent(rows_ref, count, slot):
        others = rows_ref.at[pl.ds(0, count - 1), :]
        pltpu.make_async_copy(others, others, asem.at[slot, 0]).wait()

    g = jnp.broadcast_to(jnp.sum(G[...], axis=0, keepdims=True), (8, 128))
    def faces_sent():
        for p in range(5):
            all_six(p, ssem)
        c_copy.wait_send()

    g = everyone(g, line, row_b, me[0], nx, 1, faces_sent)
    g = everyone(g, plane, row_a, me[1] * nz + me[2], ny * nz, 0, lambda: sent(row_b, nx, 1))

    ahead, after = rolled(g, -10), rolled(g, -20)
    normal = (SHIFT * SHIFT) * g + (2 * SHIFT * SCALE) * ahead + (SCALE * SCALE) * after
    right = SHIFT * g + SCALE * ahead
    entries = jnp.where(lane < 80, normal, rolled(right, 70))
    def entry(r):
        return jnp.broadcast_to(entries[:, r : r + 1], (8, 128))

    n = 16
    a = {}
    for i in range(n):
        for j in range(i + 1):
            a[i, j] = entry(10 * (i // 4 + j // 4 + 1) + PLACE[i % 4, j % 4])
    b = []
    for i in range(n):
        value = entry(80 + 10 * (i // 4) + PLACE[i % 4, 3])
        for j in range(3):
            value = jnp.where(sub == j, entry(80 + 10 * (i // 4) + PLACE[i % 4, j]), value)
        b.append(value)
    inverse = []
    for k in range(n):
        inverse.append(1.0 / a[k, k])
        for i in range(k + 1, n):
            factor = a[i, k] * inverse[k]
            for j in range(k + 1, i + 1):
                a[i, j] = a[i, j] - factor * a[j, k]
            b[i] = b[i] - factor * b[k]
    for i in reversed(range(n)):
        b[i] = b[i] * inverse[i]
        W[i, :, :] = b[i]
        for j in range(i):
            b[j] = b[j] - a[i, j] * b[i]

    def update(x, carry):
        total = [[V[0, x, f, pl.ds(TOP + 8 * t, 8), :] for t in range(4)] for f in range(4)]
        for c in range(16):
            v = [V[1 + c // 4, x, c % 4, pl.ds(TOP + 8 * t, 8), :] for t in range(4)]
            for f in range(4):
                w = jnp.broadcast_to(W[c, pl.ds(f, 1), :], (8, 128))
                for t in range(4):
                    total[f][t] = total[f][t] + w * v[t]
        for f in range(4):
            for t in range(4):
                out[f, x, pl.ds(8 * t, 8), :] = total[f][t]
        return carry

    lax.fori_loop(0, 5, update, 0)

    sent(row_a, ny * nz, 0)


def solution(mesh):
    sizes = tuple(mesh.shape[axis] for axis in AXES)
    spec = P(None, "gx", "gy", "gz")

    def local(start, rhs_block, coefficients):
        vmem = lambda *shape: pltpu.VMEM(shape, F32)
        return pl.pallas_call(
            lambda *refs: kernel(sizes, *refs),
            out_shape=jax.ShapeDtypeStruct(start.shape, F32),
            in_specs=[pl.BlockSpec(memory_space=pl.ANY)] * 3,
            out_specs=pl.BlockSpec(memory_space=pltpu.VMEM),
            scratch_shapes=[
                vmem(6, 5, 4, 48, 128), vmem(4, 5, 32, 128), vmem(4, 5, 32, 128),
                vmem(5, 32, 128), vmem(5, 32, 128), vmem(5, 48, 128),
                vmem(5, 32, 128), vmem(5, 32, 128), vmem(5, 32, 128),
                vmem(2, 32, 128), vmem(2, 5, 8, 128),
                vmem(5, 11, 32, 128), vmem(32, 128),
                vmem(5, 2, 32, 128), vmem(5, 16, 128),
                vmem(8, 128), vmem(192, 128), vmem(32, 128), vmem(16, 128), vmem(2, 8, 128), vmem(16, 8, 128),
                pltpu.SemaphoreType.DMA((6,)), pltpu.SemaphoreType.DMA((6,)),
                pltpu.SemaphoreType.DMA((6,)), pltpu.SemaphoreType.DMA((2, 2)),
            ],
            compiler_params=pltpu.CompilerParams(
                collective_id=0, has_side_effects=True, vmem_limit_bytes=54764 << 10
            ),
        )(start, rhs_block, coefficients)

    return jax.shard_map(local, mesh=mesh, in_specs=(spec,) * 3, out_specs=spec, check_vma=False)
```
